128 devices in a mesh: row: 16 (over y, x), col: 2 (over core), rhs: 4 (over z).
Axes of the slice: x: 4, y: 4, z: 4, core: 2. Of those that a mesh axis runs over, the one named last changes fastest.
Arguments:
- load_cases: bfloat16 [6, 2, 16, 256, 1024], P(None, 'col', 'row', None, 'rhs'), parts along dimension 4, may hold values from -6 to 6
- diag_inverse: bfloat16 [6, 2, 16, 256, 256], P(None, 'col', 'row')
- factor_tiles: bfloat16 [5, 2, 16, 32, 256, 256], P(None, 'col', None, 'row'), may hold values from -0.0625 to 0.0625
- targets: int32 [5, 2, 16, 32], P(None, 'col', None, 'row'), may hold values from 0 to 9, as said below
- tile_live: int32 [5, 2, 16, 32], P(None, 'col', None, 'row'), may hold values from 0 to 1, as said below
Outputs:
- solution: bfloat16 [6, 2, 16, 256, 1024], P(None, 'col', 'row', None, 'rhs'), parts along dimension 4
The draws below stay inside these ranges and needn't reach their ends.
There are 4 independent parts, one for each index of `rhs`. The reference program is written for one: setup_inputs(seed, part) draws one part's arguments, and reference() takes and returns one part's arrays. A program takes and returns all parts, laid end to end along the dimension named above; an argument that names none is the same for every part. Nothing has to cross between parts.
Inputs may be any that keep to these rules, and one draw needn't show every extreme that they name: targets[l, c, q, k] is below (5 - l) * 2, so that every block row lies in a higher level. `tile_live`: in each source level every slot of the supernodes of one index c is 1.
All inputs are finite; a program needn't handle non-finite values.
Results may differ from the reference program's by a relative error of at most 0.022.
Values may be sent and summed in bfloat16 or wider, within the bound.
No kernel may reach another device: no remote copies, remote signals or barrier semaphores. Data moves between devices by JAX's collectives and lax.ppermute only.
A program may use at most 192 MiB of HBM per device.

```python
import math
import jax
import jax.numpy as jnp

B = 256
NRHS = 256
LEV = 6
KR = 2
SLOTS = 32
N_ROW = 16
N_COL = 2


def draw_diag_inverse(key, part):
    key = jax.random.fold_in(key, 11)
    noise = jax.random.normal(key, (LEV, N_COL, N_ROW, B, B), jnp.float32) * (0.3 / math.sqrt(B))
    return (noise + jnp.eye(B, dtype=jnp.float32)).astype(jnp.bfloat16)


def draw_targets(key, part):
    key = jax.random.fold_in(key, 23)
    stacked = []
    for height in range(LEV - 1):
        level_key = jax.random.fold_in(key, height)
        stacked.append(jax.random.randint(level_key, (N_COL, N_ROW, SLOTS), 0, (LEV - 1 - height) * N_COL, jnp.int32))
    result = jnp.stack(stacked)
    result = result.at[0, 0, 0, 0].set((LEV - 1) * N_COL - 1)
    return result.at[0, 0, 0, SLOTS - 1].set(0)


def draw_tile_live(key, part):
    key = jax.random.fold_in(key, 37)
    heavy_key, coin_key = jax.random.split(key)
    heavy_col = jax.random.randint(heavy_key, (LEV - 1, 1, 1, 1), 0, N_COL, jnp.int32)
    coin_flip = jax.random.randint(coin_key, (LEV - 1, N_COL, N_ROW, SLOTS), 0, 2, jnp.int32)
    column_ids = jnp.arange(N_COL, dtype=jnp.int32).reshape(1, N_COL, 1, 1)
    return jnp.where(column_ids == heavy_col, 1, coin_flip).astype(jnp.int32)


def steps_of(key, shape, cuts, smallest, top_value):
    def one(position, blocks):
        heights = jax.random.uniform(jax.random.fold_in(jax.random.fold_in(key, 6), position), (blocks,), jnp.float32, smallest / len(cuts), top_value / len(cuts))
        return jnp.repeat(jnp.exp(heights), shape[position] // blocks).reshape((-1,) + (1,) * (len(shape) - position - 1))

    loudness = one(*cuts[0])
    for cut in cuts[1:]:
        loudness = loudness * one(*cut)
    return loudness


def gaussian(own_key, extent, spread, limit, cuts=(), held_as=jnp.bfloat16):
    gain = steps_of(own_key, extent, cuts, -0.22, 0.18) if cuts else 1.0
    array = jax.random.normal(own_key, extent, jnp.float32) * spread * gain
    return jnp.minimum(jnp.maximum(array, -limit), limit).astype(held_as)


def setup_inputs(seed: int = 0, part: int = 0) -> dict:
    keys = jax.random.split(jax.random.key(seed), 6)
    part_keys = jax.random.split(jax.random.fold_in(keys[5], part), 6)
    load_cases = gaussian(part_keys[0], (LEV, N_COL, N_ROW, B, NRHS), 1.0, 6.0, ((1, 2), (2, 16)))
    diag_inverse = draw_diag_inverse(jax.random.fold_in(keys[5], 71), part)
    factor_tiles = gaussian(keys[2], (LEV - 1, N_COL, N_ROW, SLOTS, B, B), (B * SLOTS) ** -0.5, 0.0625, ((1, 2), (3, 16)))
    targets = draw_targets(jax.random.fold_in(keys[5], 71), part)
    tile_live = draw_tile_live(jax.random.fold_in(keys[5], 71), part)
    return dict(load_cases=load_cases, diag_inverse=diag_inverse, factor_tiles=factor_tiles, targets=targets, tile_live=tile_live)


def reference(load_cases, diag_inverse, factor_tiles, targets, tile_live):
    row_owner = (jnp.arange(N_ROW * KR) // KR).astype(jnp.int32)
    count_grid = N_COL * N_ROW
    updates = jnp.zeros((LEV * count_grid, B, NRHS), jnp.float32)
    masked = jnp.where(tile_live[..., None, None] > 0, factor_tiles, jnp.zeros((), factor_tiles.dtype))
    solved = []
    for height in range(LEV):
        first_idx = height * count_grid
        incoming = updates[first_idx:first_idx + count_grid].reshape(N_COL, N_ROW, B, NRHS)
        residual = (load_cases[height].astype(jnp.float32) - incoming).astype(jnp.bfloat16)
        solved_blk = jnp.einsum('cqab,cqbn->cqan', diag_inverse[height].astype(jnp.float32), residual.astype(jnp.float32)).astype(jnp.bfloat16)
        solved.append(solved_blk)
        if height < LEV - 1:
            for column in range(N_COL):
                products = jnp.einsum('qkab,qbn->qkan', masked[height, column].astype(jnp.float32), solved_blk[column].astype(jnp.float32))
                flat_idx = (((height + 1) * N_COL + targets[height, column]) * N_ROW + row_owner[None, :]).astype(jnp.int32)
                updates = updates.at[flat_idx.reshape(-1)].add(products.reshape(-1, B, NRHS))
    x_flat = jnp.zeros((LEV * count_grid, B, NRHS), jnp.bfloat16)
    results = [None] * LEV
    for height in reversed(range(LEV)):
        if height < LEV - 1:
            back_list = []
            for column in range(N_COL):
                flat_idx = (((height + 1) * N_COL + targets[height, column]) * N_ROW + row_owner[None, :]).astype(jnp.int32)
                gathered = x_flat[flat_idx]
                back_list.append(jnp.einsum('qkab,qkan->qbn', masked[height, column].astype(jnp.float32), gathered.astype(jnp.float32)))
            back = jnp.stack(back_list)
        else:
            back = jnp.zeros((N_COL, N_ROW, B, NRHS), jnp.float32)
        rest_blk = (solved[height].astype(jnp.float32) - back).astype(jnp.bfloat16)
        answer = jnp.einsum('cqba,cqbn->cqan', diag_inverse[height].astype(jnp.float32), rest_blk.astype(jnp.float32)).astype(jnp.bfloat16)
        results[height] = answer
        first_idx = height * count_grid
        x_flat = x_flat.at[first_idx:first_idx + count_grid].set(answer.reshape(count_grid, B, NRHS))
    return jnp.stack(results)
```

```python
from functools import partial

import jax
import jax.numpy as jnp
import numpy as np
from jax import lax
from jax.experimental import pallas as pl
from jax.experimental.pallas import tpu as pltpu
from jax.sharding import Mesh, PartitionSpec as P

F32, BF16 = jnp.float32, jnp.bfloat16
AXES = ("y", "x", "col")
SHIFTS = (0, 1, 3, 2)
VMEM = pl.BlockSpec(memory_space=pltpu.VMEM)
SMEM = pl.BlockSpec(memory_space=pltpu.SMEM)
ANY = pl.BlockSpec(memory_space=pl.ANY)


def pairs(near, shift):
    out = []
    for y in range(4):
        for x in range(4):
            for c in range(2):
                on_x = (c == 0) == near
                ty, tx = (y, (x + shift) % 4) if on_x else ((y + shift) % 4, x)
                out.append(((y * 4 + x) * 2 + c, (ty * 4 + tx) * 2 + c))
    return out


def send(value, near, shift):
    return lax.ppermute(value, AXES, pairs(near, shift))


def swap_cores(value):
    return lax.ppermute(value, "col", [(0, 1), (1, 0)])


def call(body, out, in_specs, out_specs, scratch=(), aliases={}, flops=0, moved=0, limit=16):
    return pl.pallas_call(
        body,
        out_shape=out,
        in_specs=in_specs,
        out_specs=out_specs,
        scratch_shapes=list(scratch),
        input_output_aliases=aliases,
        compiler_params=pltpu.CompilerParams(vmem_limit_bytes=limit << 20),
        cost_estimate=pl.CostEstimate(flops=flops, bytes_accessed=moved, transcendentals=0),
    )


def dot(a, b):
    return jnp.dot(a, b, preferred_element_type=F32)


def fetch(tiles, level, order, first, count, buf, sems):
    copies = [
        pltpu.make_async_copy(tiles.at[level, 0, order[first + i]], buf.at[i], sems.at[i])
        for i in range(count)
    ]
    for copy in copies:
        copy.start()
    return copies


def fold_body(level, first, groups, zero, finish, *refs):
    refs = list(refs)
    order, places = refs[:2]
    blocks = refs[2 : 2 + groups]
    refs = refs[2 + groups :]
    tiles = refs.pop(0)
    if not zero:
        refs.pop(0)
    load = refs.pop(0) if finish else None
    acc = refs.pop(0)
    if finish:
        pending, outgoing = refs.pop(0), refs.pop(0)
    buf, sems = refs
    count = 4 * groups
    copies = fetch(tiles, level, order, first, count, buf, sems)
    if zero:
        acc[...] = jnp.zeros_like(acc)
    size = acc.shape[1]
    for i in range(count):
        copies[i].wait()
        product = dot(buf[i].reshape(2 * size, size), blocks[i // 4][i % 4])
        for k in range(2):
            place = places[level, first + i, k]
            acc[place] += product[k * size : (k + 1) * size]
    if finish:
        pending[...] = load[...].astype(F32) - acc[2 * level]
        outgoing[...] = acc[2 * level + 1]


def fold(level, first, order, places, blocks, tiles, acc, load=None):
    groups = len(blocks)
    size, cases = blocks[0].shape[1:]
    levels = tiles.shape[0]
    count = 4 * groups
    zero, finish = acc is None, load is not None
    out = [jax.ShapeDtypeStruct((2 * levels + 1, size, cases), F32)]
    args = [order, places, *blocks, tiles]
    specs = [SMEM, SMEM] + [VMEM] * groups + [ANY]
    aliases = {}
    if not zero:
        aliases = {len(args): 0}
        args.append(acc)
        specs.append(VMEM)
    if finish:
        args.append(load)
        specs.append(VMEM)
        out += [jax.ShapeDtypeStruct((size, cases), F32)] * 2
    return call(
        partial(fold_body, level, first, groups, zero, finish),
        out,
        specs,
        [VMEM] * len(out),
        [pltpu.VMEM((count, 2, size, size), BF16), pltpu.SemaphoreType.DMA((count,))],
        aliases,
        flops=count * 4 * size * size * cases,
        moved=count * 4 * size * size,
    )(*args)


def solve_body(pending, received, inverse, solved):
    solved[...] = dot(inverse[...], (pending[...] - received[...]).astype(BF16)).astype(BF16)


def solve(pending, received, inverse):
    return call(
        solve_body, jax.ShapeDtypeStruct(pending.shape, BF16), [VMEM] * 3, VMEM, limit=8, flops=1 << 25, moved=1 << 20
    )(pending, received, inverse)


def back_body(level, first, groups, order, places, x_rows, tiles, *refs):
    outs = refs[:groups]
    buf, sems = refs[groups:]
    count = 4 * groups
    copies = fetch(tiles, level, order, first, count, buf, sems)
    for i in range(count):
        copies[i].wait()
        total = dot(x_rows[places[level, first + i, 0]], buf[i, 0])
        total += dot(x_rows[places[level, first + i, 1]], buf[i, 1])
        outs[i // 4][i % 4] = total.astype(BF16)


def back(level, first, groups, order, places, x_rows, tiles):
    cases, size = x_rows.shape[1:]
    count = 4 * groups
    return call(
        partial(back_body, level, first, groups),
        [jax.ShapeDtypeStruct((4, cases, size), BF16)] * groups,
        [SMEM, SMEM, VMEM, ANY],
        [VMEM] * groups,
        [pltpu.VMEM((count, 2, size, size), BF16), pltpu.SemaphoreType.DMA((count,))],
        flops=count * 4 * size * size * cases,
        moved=count * 4 * size * size,
    )(order, places, x_rows, tiles)


def add_body(a, b, c, d, out):
    for i in range(4):
        total = a[i].astype(F32) + b[i].astype(F32) + c[i].astype(F32) + d[i].astype(F32)
        out[i] = total.astype(BF16)


def add_four(parts):
    shape = jax.ShapeDtypeStruct(parts[0].shape, BF16)
    return call(add_body, shape, [VMEM] * 4, VMEM, limit=8, flops=1 << 20, moved=1 << 21)(*parts)


def answer_body(solved, own, a, b, c, inverse, out):
    term = own[0].astype(F32) + a[...].astype(F32) + b[...].astype(F32) + c[...].astype(F32)
    out[...] = dot((solved[...].astype(F32) - term).astype(BF16), inverse[...]).astype(BF16)


def answer(solved, own, received, inverse):
    shape = jax.ShapeDtypeStruct(solved.shape, BF16)
    return call(answer_body, shape, [VMEM] * 6, VMEM, limit=8, flops=1 << 25, moved=1 << 20)(
        solved, own, *received, inverse
    )


def shards(load_cases, diag_inverse, factor_tiles, targets, tile_live):
    levels = load_cases.shape[0]
    size, cases = load_cases.shape[3:]
    y, x, c = (lax.axis_index(name) for name in AXES)
    shifts = jnp.array(SHIFTS, jnp.int32)
    far, near = shifts[:, None], shifts[None, :]

    def order_of(sign):
        ys = jnp.where(c == 0, y + sign * far + 0 * near, y + sign * near + 0 * far) % 4
        xs = jnp.where(c == 0, x + sign * near + 0 * far, x + sign * far + 0 * near) % 4
        return (ys * 4 + xs).reshape(-1)

    level_ids = jnp.arange(levels - 1, dtype=jnp.int32)[:, None, None]
    owner = targets[:, 0]
    places = 2 * (level_ids + owner // 2) + ((owner % 2) ^ c)
    places = jnp.where(tile_live[:, 0] > 0, places, 2 * (levels - 1))
    order_in, order_out = order_of(-1), order_of(1)
    places_in, places_out = places[:, order_in], places[:, order_out]
    inverse = [diag_inverse[h, 0, 0] for h in range(levels)]
    load = [load_cases[h, 0, 0] for h in range(levels)]

    solved = [dot(inverse[0], load[0]).astype(BF16)]
    acc = None
    for height in range(levels - 1):
        mine = solved[height]
        group = jnp.stack([mine] + [send(mine, True, s) for s in SHIFTS[1:]])
        far_groups = [send(group, False, s) for s in SHIFTS[1:]]
        (acc,) = fold(height, 0, order_in, places_in, [group], factor_tiles, acc)
        acc, pending, outgoing = fold(
            height, 4, order_in, places_in, far_groups, factor_tiles, acc, load[height + 1]
        )
        solved.append(solve(pending, swap_cores(outgoing), inverse[height + 1]))

    results = [None] * levels
    x_rows = jnp.zeros((2 * levels - 1, cases, size), BF16)
    latest = lax.dot_general(
        solved[-1], inverse[-1], (((0,), (0,)), ((), ())), preferred_element_type=F32
    ).astype(BF16)
    results[-1] = latest.T
    for height in reversed(range(levels - 1)):
        x_rows = x_rows.at[2 * height].set(latest).at[2 * height + 1].set(swap_cores(latest))
        parts = back(height, 4, 3, order_out, places_out, x_rows, factor_tiles)
        moved = [send(part, False, s) for part, s in zip(parts, SHIFTS[1:])]
        (kept,) = back(height, 0, 1, order_out, places_out, x_rows, factor_tiles)
        group = add_four([kept] + moved)
        received = [send(group[i], True, SHIFTS[i]) for i in range(1, 4)]
        latest = answer(solved[height].T, group, received, inverse[height])
        results[height] = latest.T
    return jnp.stack(results)[:, None, None]


def solution(mesh):
    devices = mesh.devices
    split = Mesh(devices.reshape((4, 4) + devices.shape[1:]), ("y", "x", "col", "rhs"))
    row = ("y", "x")
    return jax.shard_map(
        shards,
        mesh=split,
        in_specs=(
            P(None, "col", row, None, "rhs"),
            P(None, "col", row, None, None),
            P(None, "col", None, row, None, None),
            P(None, "col", None, row),
            P(None, "col", None, row),
        ),
        out_specs=P(None, "col", row, None, "rhs"),
        check_vma=False,
    )
```

```python
from functools import partial

import jax
import jax.numpy as jnp
import numpy as np
from jax import lax
from jax.experimental import pallas as pl
from jax.experimental.pallas import tpu as pltpu
from jax.sharding import Mesh, PartitionSpec as P

F32, BF16 = jnp.float32, jnp.bfloat16
AXES = ("y", "x", "col")
SHIFTS = (0, 1, 3, 2)
VMEM = pl.BlockSpec(memory_space=pltpu.VMEM)
SMEM = pl.BlockSpec(memory_space=pltpu.SMEM)
HBM = pl.BlockSpec(memory_space=pltpu.HBM)


def pairs(near, shift):
    out = []
    for y in range(4):
        for x in range(4):
            for c in range(2):
                on_x = (c == 0) == near
                ty, tx = (y, (x + shift) % 4) if on_x else ((y + shift) % 4, x)
                out.append(((y * 4 + x) * 2 + c, (ty * 4 + tx) * 2 + c))
    return out


def send(value, near, shift):
    return lax.ppermute(value, AXES, pairs(near, shift))


def swap_cores(value):
    return lax.ppermute(value, "col", [(0, 1), (1, 0)])


def call(body, out, in_specs, out_specs, scratch=(), aliases={}, flops=0, moved=0, limit=40):
    return pl.pallas_call(
        body,
        out_shape=out,
        in_specs=in_specs,
        out_specs=out_specs,
        scratch_shapes=list(scratch),
        input_output_aliases=aliases,
        compiler_params=pltpu.CompilerParams(vmem_limit_bytes=limit << 20),
        cost_estimate=pl.CostEstimate(flops=flops, bytes_accessed=moved, transcendentals=0),
    )


def dot(a, b):
    return jnp.dot(a, b, preferred_element_type=F32)


def fetch(tiles, level, order, first, count, buf, sems, base=0):
    copies = [
        pltpu.make_async_copy(tiles.at[level, 0, order[first + i]], buf.at[i], sems.at[base + i])
        for i in range(count)
    ]
    for copy in copies:
        copy.start()
    return copies


def bring(source, level, target, sem):
    copy = pltpu.make_async_copy(source.at[level, 0, 0], target, sem)
    copy.start()
    return copy


def first_body(loads, inverses, solved, load, inverse, sems):
    copies = [bring(loads, 0, load, sems.at[0]), bring(inverses, 0, inverse, sems.at[1])]
    for copy in copies:
        copy.wait()
    solved[...] = dot(inverse[...], load[...]).astype(BF16)


def solve_first(loads, inverses):
    shape = loads.shape[3:]
    return call(
        first_body,
        jax.ShapeDtypeStruct(shape, BF16),
        [HBM] * 2,
        VMEM,
        [pltpu.VMEM(shape, BF16), pltpu.VMEM(inverses.shape[3:], BF16), pltpu.SemaphoreType.DMA((2,))],
        flops=1 << 25,
        moved=1 << 19,
    )(loads, inverses)


def add_products(places, base, blocks, buf, acc):
    size = acc.shape[1]
    for i in range(4 * len(blocks)):
        product = dot(buf[i].reshape(2 * size, size), blocks[i // 4][i % 4])
        for k in range(2):
            acc[places[base + 2 * i + k]] += product[k * size : (k + 1) * size]


def near_fold_body(level, zero, after, *refs):
    refs = list(refs)
    order, places, block, tiles, loads, inverses = refs[:6]
    refs = refs[6:]
    if not zero:
        refs.pop(0)
    acc, ahead, load, inverse = refs[:4]
    buf, sems = refs[-2:]
    copies = fetch(tiles, level, order, 0, 4, buf, sems)
    later = fetch(tiles, level, order, 4, 12, ahead, sems, 4)
    later.append(bring(loads, level + 1, load, sems.at[28]))
    later.append(bring(inverses, level + 1, inverse, sems.at[29]))
    if after:
        later += fetch(tiles, level, order, 20, 12, refs[4], sems, 16)
    if zero:
        acc[...] = jnp.zeros_like(acc)
    for copy in copies:
        copy.wait()
    add_products(places, 64 * level, [block], buf, acc)
    for copy in later:
        copy.wait()


def near_fold(level, order, places, block, tiles, loads, inverses, acc, after):
    size, cases = block.shape[1:]
    levels = tiles.shape[0]
    zero = acc is None
    out = [
        jax.ShapeDtypeStruct((2 * levels + 1, size, cases), F32),
        jax.ShapeDtypeStruct((12, 2, size, size), BF16),
        jax.ShapeDtypeStruct((size, cases), BF16),
        jax.ShapeDtypeStruct((size, size), BF16),
    ]
    if after:
        out.append(out[1])
    args = [order, places, block, tiles, loads, inverses]
    specs = [SMEM, SMEM, VMEM, HBM, HBM, HBM]
    if not zero:
        args.append(acc)
        specs.append(VMEM)
    return call(
        partial(near_fold_body, level, zero, after),
        out,
        specs,
        [VMEM] * len(out),
        [pltpu.VMEM((4, 2, size, size), BF16), pltpu.SemaphoreType.DMA((30,))],
        {} if zero else {6: 0},
        flops=16 * size * size * cases,
        moved=64 * size * size,
    )(*args)


def far_fold_body(level, places, a, b, c, tiles, load, _, acc, pending, outgoing):
    add_products(places, 64 * level + 8, [a, b, c], tiles, acc)
    pending[...] = load[...].astype(F32) - acc[2 * level]
    outgoing[...] = acc[2 * level + 1]


def far_fold(level, places, blocks, tiles, load, acc):
    size, cases = load.shape
    half = jax.ShapeDtypeStruct((size, cases), F32)
    return call(
        partial(far_fold_body, level),
        [jax.ShapeDtypeStruct(acc.shape, F32), half, half],
        [SMEM] + [VMEM] * 6,
        [VMEM] * 3,
        aliases={6: 0},
        limit=16,
        flops=48 * size * size * cases,
        moved=1 << 20,
    )(places, *blocks, tiles, load, acc)


def solve_body(pending, received, inverse, solved):
    solved[...] = dot(inverse[...], (pending[...] - received[...]).astype(BF16)).astype(BF16)


def solve_last_body(pending, received, inverse, answered):
    solved = dot(inverse[...], (pending[...] - received[...]).astype(BF16)).astype(BF16)
    answered[...] = lax.dot_general(
        solved, inverse[...], (((0,), (0,)), ((), ())), preferred_element_type=F32
    ).astype(BF16)


def solve(body, pending, received, inverse):
    shape = jax.ShapeDtypeStruct(pending.shape, BF16)
    return call(body, shape, [VMEM] * 3, VMEM, limit=8, flops=1 << 25, moved=1 << 20)(
        pending, received, inverse
    )


def back_product(places, slot, x_rows, pair):
    total = dot(x_rows[places[slot]], pair[0])
    return (total + dot(x_rows[places[slot + 1]], pair[1])).astype(BF16)


def far_back_body(level, zero, places, own, other, tiles, *refs):
    x_rows, outs = refs[-4], refs[-3:]
    if zero:
        x_rows[x_rows.shape[0] - 1] = jnp.zeros_like(own)
    x_rows[2 * level] = own[...]
    x_rows[2 * level + 1] = other[...]
    for i in range(12):
        outs[i // 4][i % 4] = back_product(places, 64 * level + 40 + 2 * i, x_rows, tiles[i])


def far_back(level, levels, places, own, other, tiles, x_rows):
    cases, size = own.shape
    zero = x_rows is None
    part = jax.ShapeDtypeStruct((4, cases, size), BF16)
    args = [places, own, other, tiles] + ([] if zero else [x_rows])
    return call(
        partial(far_back_body, level, zero),
        [jax.ShapeDtypeStruct((2 * levels - 1, cases, size), BF16), part, part, part],
        [SMEM] + [VMEM] * (len(args) - 1),
        [VMEM] * 4,
        aliases={} if zero else {4: 0},
        limit=16,
        flops=48 * size * size * cases,
        moved=1 << 20,
    )(*args)


def near_back_body(level, order, places, x_rows, solved, tiles, inverses, out, turned, inverse, *refs):
    buf, sems = refs[-2:]
    copies = fetch(tiles, level, order, 16, 4, buf, sems)
    later = [bring(inverses, level, inverse, sems.at[16])]
    if level:
        later += fetch(tiles, level - 1, order, 20, 12, refs[0], sems, 4)
    turned[...] = solved[...].T
    for copy in copies:
        copy.wait()
    for i in range(4):
        out[i] = back_product(places, 64 * level + 32 + 2 * i, x_rows, buf[i])
    for copy in later:
        copy.wait()


def near_back(level, order, places, x_rows, solved, tiles, inverses):
    cases, size = x_rows.shape[1:]
    out = [
        jax.ShapeDtypeStruct((4, cases, size), BF16),
        jax.ShapeDtypeStruct((cases, size), BF16),
        jax.ShapeDtypeStruct((size, size), BF16),
    ]
    if level:
        out.append(jax.ShapeDtypeStruct((12, 2, size, size), BF16))
    return call(
        partial(near_back_body, level),
        out,
        [SMEM, SMEM, VMEM, VMEM, HBM, HBM],
        [VMEM] * len(out),
        [pltpu.VMEM((4, 2, size, size), BF16), pltpu.SemaphoreType.DMA((17,))],
        flops=16 * size * size * cases,
        moved=64 * size * size,
    )(order, places, x_rows, solved, tiles, inverses)


def add_body(a, b, c, d, *outs):
    for i in range(4):
        total = a[i].astype(F32) + b[i].astype(F32) + c[i].astype(F32) + d[i].astype(F32)
        outs[i][...] = total.astype(BF16)


def add_four(parts):
    shape = jax.ShapeDtypeStruct(parts[0].shape[1:], BF16)
    return call(add_body, [shape] * 4, [VMEM] * 4, [VMEM] * 4, limit=8, flops=1 << 20, moved=1 << 21)(*parts)


def answer_body(solved, own, a, b, c, inverse, out):
    term = own[...].astype(F32) + a[...].astype(F32) + b[...].astype(F32) + c[...].astype(F32)
    out[...] = dot((solved[...].astype(F32) - term).astype(BF16), inverse[...]).astype(BF16)


def answer(solved, own, received, inverse):
    shape = jax.ShapeDtypeStruct(solved.shape, BF16)
    return call(answer_body, shape, [VMEM] * 6, VMEM, limit=8, flops=1 << 25, moved=1 << 20)(
        solved, own, *received, inverse
    )


def shards(load_cases, diag_inverse, factor_tiles, targets, tile_live):
    levels = load_cases.shape[0]
    size, cases = load_cases.shape[3:]
    y, x, c = (lax.axis_index(name) for name in AXES)
    shifts = jnp.array(SHIFTS, jnp.int32)
    far, near = shifts[:, None], shifts[None, :]

    def order_of(sign):
        ys = jnp.where(c == 0, y + sign * far + 0 * near, y + sign * near + 0 * far) % 4
        xs = jnp.where(c == 0, x + sign * near + 0 * far, x + sign * far + 0 * near) % 4
        return (ys * 4 + xs).reshape(-1)

    level_ids = jnp.arange(levels - 1, dtype=jnp.int32)[:, None, None]
    owner = targets[:, 0]
    places = 2 * (level_ids + owner // 2) + ((owner % 2) ^ c)
    places = jnp.where(tile_live[:, 0] > 0, places, 2 * (levels - 1))
    order = jnp.concatenate([order_of(-1), order_of(1)])
    places = places[:, order].reshape(-1)

    solved = [solve_first(load_cases, diag_inverse)]
    acc = None
    for height in range(levels - 1):
        mine = solved[height]
        group = jnp.stack([mine] + [send(mine, True, s) for s in SHIFTS[1:]])
        far_groups = [send(group, False, s) for s in SHIFTS[1:]]
        last = height == levels - 2
        acc, ahead, load, inverse, *rest = near_fold(
            height, order, places, group, factor_tiles, load_cases, diag_inverse, acc, last
        )
        acc, pending, outgoing = far_fold(height, places, far_groups, ahead, load, acc)
        body = solve_last_body if last else solve_body
        solved.append(solve(body, pending, swap_cores(outgoing), inverse))

    latest = solved[-1]
    results = [latest]
    x_rows = None
    for height in reversed(range(levels - 1)):
        x_rows, *parts = far_back(
            height, levels, places, latest, swap_cores(latest), rest[0], x_rows
        )
        moved = [send(part, False, s) for part, s in zip(parts, SHIFTS[1:])]
        kept, turned, inverse, *rest = near_back(
            height, order, places, x_rows, solved[height], factor_tiles, diag_inverse
        )
        own, *others = add_four([kept] + moved)
        received = [send(other, True, s) for other, s in zip(others, SHIFTS[1:])]
        latest = answer(turned, own, received, inverse)
        results.append(latest)
    results = lax.optimization_barrier(tuple(reversed(results)))
    return jnp.stack([result.T for result in results])[:, None, None]


def solution(mesh):
    devices = mesh.devices
    split = Mesh(devices.reshape((4, 4) + devices.shape[1:]), ("y", "x", "col", "rhs"))
    row = ("y", "x")
    return jax.shard_map(
        shards,
        mesh=split,
        in_specs=(
            P(None, "col", row, None, "rhs"),
            P(None, "col", row, None, None),
            P(None, "col", None, row, None, None),
            P(None, "col", None, row),
            P(None, "col", None, row),
        ),
        out_specs=P(None, "col", row, None, "rhs"),
        check_vma=False,
    )
```

```python
from functools import partial

import jax
import jax.numpy as jnp
import numpy as np
from jax import lax
from jax.experimental import pallas as pl
from jax.experimental.pallas import tpu as pltpu
from jax.sharding import Mesh, PartitionSpec as P

F32, BF16 = jnp.float32, jnp.bfloat16
AXES = ("y", "x", "col")
IN = (0, 1, 3, 2)
OUT = (0, 2, 1, 3)
VMEM = pl.BlockSpec(memory_space=pltpu.VMEM)
SMEM = pl.BlockSpec(memory_space=pltpu.SMEM)
HBM = pl.BlockSpec(memory_space=pltpu.HBM)


def pairs(near, shift):
    out = []
    for y in range(4):
        for x in range(4):
            for c in range(2):
                on_x = (c == 0) == near
                ty, tx = (y, (x + shift) % 4) if on_x else ((y + shift) % 4, x)
                out.append(((y * 4 + x) * 2 + c, (ty * 4 + tx) * 2 + c))
    return out


def send(value, near, shift):
    return lax.ppermute(value, AXES, pairs(near, shift))


def swap_cores(value):
    return lax.ppermute(value, "col", [(0, 1), (1, 0)])


def call(body, out, in_specs, out_specs, scratch=(), aliases={}, flops=0, moved=0, limit=40):
    return pl.pallas_call(
        body,
        out_shape=out,
        in_specs=in_specs,
        out_specs=out_specs,
        scratch_shapes=list(scratch),
        input_output_aliases=aliases,
        compiler_params=pltpu.CompilerParams(vmem_limit_bytes=limit << 20),
        cost_estimate=pl.CostEstimate(flops=flops, bytes_accessed=moved, transcendentals=0),
    )


def dot(a, b):
    return jnp.dot(a, b, preferred_element_type=F32)


def fetch(tiles, level, order, first, count, buf, sems, base=0):
    copies = [
        pltpu.make_async_copy(tiles.at[level, 0, order[first + i]], buf.at[i], sems.at[base + i])
        for i in range(count)
    ]
    for copy in copies:
        copy.start()
    return copies


def bring(source, level, target, sem):
    copy = pltpu.make_async_copy(source.at[level, 0, 0], target, sem)
    copy.start()
    return copy


def first_body(loads, inverses, solved, load, inverse, sems):
    copies = [bring(loads, 0, load, sems.at[0]), bring(inverses, 0, inverse, sems.at[1])]
    for copy in copies:
        copy.wait()
    solved[...] = dot(inverse[...], load[...]).astype(BF16)


def solve_first(loads, inverses):
    shape = loads.shape[3:]
    return call(
        first_body,
        jax.ShapeDtypeStruct(shape, BF16),
        [HBM] * 2,
        VMEM,
        [pltpu.VMEM(shape, BF16), pltpu.VMEM(inverses.shape[3:], BF16), pltpu.SemaphoreType.DMA((2,))],
        flops=1 << 25,
        moved=1 << 19,
    )(loads, inverses)


def add_products(places, base, blocks, buf, acc):
    size = acc.shape[1]
    for i in range(4 * len(blocks)):
        product = dot(buf[i].reshape(2 * size, size), blocks[i // 4][i % 4])
        for k in range(2):
            acc[places[base + 2 * i + k]] += product[k * size : (k + 1) * size]


def near_fold_body(level, zero, after, *refs):
    refs = list(refs)
    order, places, block, tiles, loads, inverses = refs[:6]
    refs = refs[6:]
    if not zero:
        refs.pop(0)
    acc, ahead, load, inverse = refs[:4]
    buf, sems = refs[-2:]
    copies = fetch(tiles, level, order, 0, 4, buf, sems)
    later = fetch(tiles, level, order, 4, 12, ahead, sems, 4)
    later.append(bring(loads, level + 1, load, sems.at[28]))
    later.append(bring(inverses, level + 1, inverse, sems.at[29]))
    if after:
        later += fetch(tiles, level, order, 20, 12, refs[4], sems, 16)
    if zero:
        acc[...] = jnp.zeros_like(acc)
    for copy in copies:
        copy.wait()
    add_products(places, 64 * level, [block], buf, acc)
    for copy in later:
        copy.wait()


def near_fold(level, order, places, block, tiles, loads, inverses, acc, after):
    size, cases = block.shape[1:]
    levels = tiles.shape[0]
    zero = acc is None
    out = [
        jax.ShapeDtypeStruct((2 * levels + 1, size, cases), F32),
        jax.ShapeDtypeStruct((12, 2, size, size), BF16),
        jax.ShapeDtypeStruct((size, cases), BF16),
        jax.ShapeDtypeStruct((size, size), BF16),
    ]
    if after:
        out.append(out[1])
    args = [order, places, block, tiles, loads, inverses]
    specs = [SMEM, SMEM, VMEM, HBM, HBM, HBM]
    if not zero:
        args.append(acc)
        specs.append(VMEM)
    return call(
        partial(near_fold_body, level, zero, after),
        out,
        specs,
        [VMEM] * len(out),
        [pltpu.VMEM((4, 2, size, size), BF16), pltpu.SemaphoreType.DMA((30,))],
        {} if zero else {6: 0},
        flops=16 * size * size * cases,
        moved=64 * size * size,
    )(*args)


def far_fold_body(level, places, a, b, c, tiles, load, _, acc, pending, outgoing):
    add_products(places, 64 * level + 8, [a, b, c], tiles, acc)
    pending[...] = load[...].astype(F32) - acc[2 * level]
    outgoing[...] = acc[2 * level + 1]


def far_fold(level, places, blocks, tiles, load, acc):
    size, cases = load.shape
    half = jax.ShapeDtypeStruct((size, cases), F32)
    return call(
        partial(far_fold_body, level),
        [jax.ShapeDtypeStruct(acc.shape, F32), half, half],
        [SMEM] + [VMEM] * 6,
        [VMEM] * 3,
        aliases={6: 0},
        limit=16,
        flops=48 * size * size * cases,
        moved=1 << 20,
    )(places, *blocks, tiles, load, acc)


def solve_body(pending, received, inverse, solved):
    solved[...] = dot(inverse[...], (pending[...] - received[...]).astype(BF16)).astype(BF16)


def solve_last_body(pending, received, inverse, answered):
    solved = dot(inverse[...], (pending[...] - received[...]).astype(BF16)).astype(BF16)
    answered[...] = lax.dot_general(
        solved, inverse[...], (((0,), (0,)), ((), ())), preferred_element_type=F32
    ).astype(BF16)


def solve(body, pending, received, inverse):
    shape = jax.ShapeDtypeStruct(pending.shape, BF16)
    return call(body, shape, [VMEM] * 3, VMEM, limit=8, flops=1 << 25, moved=1 << 20)(
        pending, received, inverse
    )


def back_product(places, slot, x_rows, pair):
    total = dot(x_rows[places[slot]], pair[0])
    return (total + dot(x_rows[places[slot + 1]], pair[1])).astype(BF16)


def far_back_body(level, zero, places, own, other, tiles, *refs):
    x_rows, outs = refs[-4], refs[-3:]
    if zero:
        x_rows[x_rows.shape[0] - 1] = jnp.zeros_like(own)
    x_rows[2 * level] = own[...]
    x_rows[2 * level + 1] = other[...]
    for i in range(12):
        outs[i // 4][i % 4] = back_product(places, 64 * level + 40 + 2 * i, x_rows, tiles[i])


def far_back(level, levels, places, own, other, tiles, x_rows):
    cases, size = own.shape
    zero = x_rows is None
    part = jax.ShapeDtypeStruct((4, cases, size), BF16)
    args = [places, own, other, tiles] + ([] if zero else [x_rows])
    return call(
        partial(far_back_body, level, zero),
        [jax.ShapeDtypeStruct((2 * levels - 1, cases, size), BF16), part, part, part],
        [SMEM] + [VMEM] * (len(args) - 1),
        [VMEM] * 4,
        aliases={} if zero else {4: 0},
        limit=16,
        flops=48 * size * size * cases,
        moved=1 << 20,
    )(*args)


def near_back_body(level, order, places, x_rows, solved, tiles, inverses, out, turned, inverse, *refs):
    buf, sems = refs[-2:]
    copies = fetch(tiles, level, order, 16, 4, buf, sems)
    later = [bring(inverses, level, inverse, sems.at[16])]
    if level:
        later += fetch(tiles, level - 1, order, 20, 12, refs[0], sems, 4)
    turned[...] = solved[...].T
    for copy in copies:
        copy.wait()
    for i in range(4):
        out[i] = back_product(places, 64 * level + 32 + 2 * i, x_rows, buf[i])
    for copy in later:
        copy.wait()


def near_back(level, order, places, x_rows, solved, tiles, inverses):
    cases, size = x_rows.shape[1:]
    out = [
        jax.ShapeDtypeStruct((4, cases, size), BF16),
        jax.ShapeDtypeStruct((cases, size), BF16),
        jax.ShapeDtypeStruct((size, size), BF16),
    ]
    if level:
        out.append(jax.ShapeDtypeStruct((12, 2, size, size), BF16))
    return call(
        partial(near_back_body, level),
        out,
        [SMEM, SMEM, VMEM, VMEM, HBM, HBM],
        [VMEM] * len(out),
        [pltpu.VMEM((4, 2, size, size), BF16), pltpu.SemaphoreType.DMA((17,))],
        flops=16 * size * size * cases,
        moved=64 * size * size,
    )(order, places, x_rows, solved, tiles, inverses)


def add_body(a, b, c, d, *outs):
    for i in range(4):
        total = a[i].astype(F32) + b[i].astype(F32) + c[i].astype(F32) + d[i].astype(F32)
        outs[i][...] = total.astype(BF16)


def add_four(parts):
    shape = jax.ShapeDtypeStruct(parts[0].shape[1:], BF16)
    return call(add_body, [shape] * 4, [VMEM] * 4, [VMEM] * 4, limit=8, flops=1 << 20, moved=1 << 21)(*parts)


def answer_body(solved, own, a, b, c, inverse, out):
    term = own[...].astype(F32) + a[...].astype(F32) + b[...].astype(F32) + c[...].astype(F32)
    out[...] = dot((solved[...].astype(F32) - term).astype(BF16), inverse[...]).astype(BF16)


def answer(solved, own, received, inverse):
    shape = jax.ShapeDtypeStruct(solved.shape, BF16)
    return call(answer_body, shape, [VMEM] * 6, VMEM, limit=8, flops=1 << 25, moved=1 << 20)(
        solved, own, *received, inverse
    )


def shards(load_cases, diag_inverse, factor_tiles, targets, tile_live):
    levels = load_cases.shape[0]
    size, cases = load_cases.shape[3:]
    y, x, c = (lax.axis_index(name) for name in AXES)

    def order_of(sign, shifts):
        far, near = jnp.array(shifts, jnp.int32)[:, None], jnp.array(shifts, jnp.int32)[None, :]
        ys = jnp.where(c == 0, y + sign * far + 0 * near, y + sign * near + 0 * far) % 4
        xs = jnp.where(c == 0, x + sign * near + 0 * far, x + sign * far + 0 * near) % 4
        return (ys * 4 + xs).reshape(-1)

    level_ids = jnp.arange(levels - 1, dtype=jnp.int32)[:, None, None]
    owner = targets[:, 0]
    places = 2 * (level_ids + owner // 2) + ((owner % 2) ^ c)
    places = jnp.where(tile_live[:, 0] > 0, places, 2 * (levels - 1))
    order = jnp.concatenate([order_of(-1, IN), order_of(1, OUT)])
    places = places[:, order].reshape(-1)

    solved = [solve_first(load_cases, diag_inverse)]
    acc = None
    for height in range(levels - 1):
        mine = solved[height]
        group = jnp.stack([mine] + [send(mine, True, s) for s in IN[1:]])
        far_groups = [send(group, False, s) for s in IN[1:]]
        last = height == levels - 2
        acc, ahead, load, inverse, *rest = near_fold(
            height, order, places, group, factor_tiles, load_cases, diag_inverse, acc, last
        )
        acc, pending, outgoing = far_fold(height, places, far_groups, ahead, load, acc)
        body = solve_last_body if last else solve_body
        solved.append(solve(body, pending, swap_cores(outgoing), inverse))

    latest = solved[-1]
    results = [latest]
    x_rows = None
    for height in reversed(range(levels - 1)):
        x_rows, *parts = far_back(
            height, levels, places, latest, swap_cores(latest), rest[0], x_rows
        )
        moved = [send(part, False, s) for part, s in zip(parts, OUT[1:])]
        kept, turned, inverse, *rest = near_back(
            height, order, places, x_rows, solved[height], factor_tiles, diag_inverse
        )
        own, *others = add_four([kept] + moved)
        received = [send(other, True, s) for other, s in zip(others, OUT[1:])]
        latest = answer(turned, own, received, inverse)
        results.append(latest)
    results = lax.optimization_barrier(tuple(reversed(results)))
    return jnp.stack([result.T for result in results])[:, None, None]


def solution(mesh):
    devices = mesh.devices
    split = Mesh(devices.reshape((4, 4) + devices.shape[1:]), ("y", "x", "col", "rhs"))
    row = ("y", "x")
    return jax.shard_map(
        shards,
        mesh=split,
        in_specs=(
            P(None, "col", row, None, "rhs"),
            P(None, "col", row, None, None),
            P(None, "col", None, row, None, None),
            P(None, "col", None, row),
            P(None, "col", None, row),
        ),
        out_specs=P(None, "col", row, None, "rhs"),
        check_vma=False,
    )
```

```python
from functools import partial

import jax
import jax.numpy as jnp
import numpy as np
from jax import lax
from jax.experimental import pallas as pl
from jax.experimental.pallas import tpu as pltpu
from jax.sharding import Mesh, PartitionSpec as P

F32, BF16 = jnp.float32, jnp.bfloat16
AXES = ("y", "x", "col")
NEAR = (0, 2, 1, 3)
FAR = (0, 1, 3, 2)
OUT = (0, 2, 1, 3)
VMEM = pl.BlockSpec(memory_space=pltpu.VMEM)
SMEM = pl.BlockSpec(memory_space=pltpu.SMEM)
HBM = pl.BlockSpec(memory_space=pltpu.HBM)


def pairs(near, shift):
    out = []
    for y in range(4):
        for x in range(4):
            for c in range(2):
                on_x = (c == 0) == near
                ty, tx = (y, (x + shift) % 4) if on_x else ((y + shift) % 4, x)
                out.append(((y * 4 + x) * 2 + c, (ty * 4 + tx) * 2 + c))
    return out


def send(value, near, shift):
    return lax.ppermute(value, AXES, pairs(near, shift))


def swap_cores(value):
    return lax.ppermute(value, "col", [(0, 1), (1, 0)])


def call(body, out, in_specs, out_specs, scratch=(), aliases={}, flops=0, moved=0, limit=40):
    return pl.pallas_call(
        body,
        out_shape=out,
        in_specs=in_specs,
        out_specs=out_specs,
        scratch_shapes=list(scratch),
        input_output_aliases=aliases,
        compiler_params=pltpu.CompilerParams(vmem_limit_bytes=limit << 20),
        cost_estimate=pl.CostEstimate(flops=flops, bytes_accessed=moved, transcendentals=0),
    )


def dot(a, b):
    return jnp.dot(a, b, preferred_element_type=F32)


def fetch(tiles, level, order, first, count, buf, sems, base=0):
    copies = [
        pltpu.make_async_copy(tiles.at[level, 0, order[first + i]], buf.at[i], sems.at[base + i])
        for i in range(count)
    ]
    for copy in copies:
        copy.start()
    return copies


def bring(source, level, target, sem):
    copy = pltpu.make_async_copy(source.at[level, 0, 0], target, sem)
    copy.start()
    return copy


def first_body(loads, inverses, solved, load, inverse, sems):
    copies = [bring(loads, 0, load, sems.at[0]), bring(inverses, 0, inverse, sems.at[1])]
    for copy in copies:
        copy.wait()
    solved[...] = dot(inverse[...], load[...]).astype(BF16)


def solve_first(loads, inverses):
    shape = loads.shape[3:]
    return call(
        first_body,
        jax.ShapeDtypeStruct(shape, BF16),
        [HBM] * 2,
        VMEM,
        [pltpu.VMEM(shape, BF16), pltpu.VMEM(inverses.shape[3:], BF16), pltpu.SemaphoreType.DMA((2,))],
        flops=1 << 25,
        moved=1 << 19,
    )(loads, inverses)


def add_products(places, base, blocks, buf, acc):
    size = acc.shape[1]
    for i in range(4 * len(blocks)):
        product = dot(buf[i].reshape(2 * size, size), blocks[i // 4][i % 4])
        for k in range(2):
            acc[places[base + 2 * i + k]] += product[k * size : (k + 1) * size]


def near_fold_body(level, zero, after, *refs):
    refs = list(refs)
    order, places, block, tiles, loads, inverses = refs[:6]
    refs = refs[6:]
    if not zero:
        refs.pop(0)
    acc, ahead, load, inverse = refs[:4]
    buf, sems = refs[-2:]
    copies = fetch(tiles, level, order, 0, 4, buf, sems)
    later = fetch(tiles, level, order, 4, 12, ahead, sems, 4)
    later.append(bring(loads, level + 1, load, sems.at[28]))
    later.append(bring(inverses, level + 1, inverse, sems.at[29]))
    if after:
        later += fetch(tiles, level, order, 20, 12, refs[4], sems, 16)
    if zero:
        acc[...] = jnp.zeros_like(acc)
    for copy in copies:
        copy.wait()
    add_products(places, 64 * level, [block], buf, acc)
    for copy in later:
        copy.wait()


def near_fold(level, order, places, block, tiles, loads, inverses, acc, after):
    size, cases = block.shape[1:]
    levels = tiles.shape[0]
    zero = acc is None
    out = [
        jax.ShapeDtypeStruct((2 * levels + 1, size, cases), F32),
        jax.ShapeDtypeStruct((12, 2, size, size), BF16),
        jax.ShapeDtypeStruct((size, cases), BF16),
        jax.ShapeDtypeStruct((size, size), BF16),
    ]
    if after:
        out.append(out[1])
    args = [order, places, block, tiles, loads, inverses]
    specs = [SMEM, SMEM, VMEM, HBM, HBM, HBM]
    if not zero:
        args.append(acc)
        specs.append(VMEM)
    return call(
        partial(near_fold_body, level, zero, after),
        out,
        specs,
        [VMEM] * len(out),
        [pltpu.VMEM((4, 2, size, size), BF16), pltpu.SemaphoreType.DMA((30,))],
        {} if zero else {6: 0},
        flops=16 * size * size * cases,
        moved=64 * size * size,
    )(*args)


def mid_fold_body(level, places, block, tiles, _, acc):
    add_products(places, 64 * level + 24, [block], tiles.at[8:12], acc)


def mid_fold(level, places, block, tiles, acc):
    size = block.shape[1]
    return call(
        partial(mid_fold_body, level),
        jax.ShapeDtypeStruct(acc.shape, F32),
        [SMEM] + [VMEM] * 3,
        VMEM,
        aliases={3: 0},
        limit=16,
        flops=16 * size * size * size,
        moved=1 << 20,
    )(places, block, tiles, acc)


def far_fold_body(level, places, a, b, tiles, load, _, acc, pending, outgoing):
    add_products(places, 64 * level + 8, [a, b], tiles, acc)
    pending[...] = load[...].astype(F32) - acc[2 * level]
    outgoing[...] = acc[2 * level + 1].astype(BF16)


def far_fold(level, places, blocks, tiles, load, acc):
    size, cases = load.shape
    half = jax.ShapeDtypeStruct((size, cases), F32)
    return call(
        partial(far_fold_body, level),
        [jax.ShapeDtypeStruct(acc.shape, F32), half, jax.ShapeDtypeStruct((size, cases), BF16)],
        [SMEM] + [VMEM] * 5,
        [VMEM] * 3,
        aliases={5: 0},
        limit=16,
        flops=48 * size * size * cases,
        moved=1 << 20,
    )(places, *blocks, tiles, load, acc)


def solve_body(pending, received, inverse, solved):
    solved[...] = dot(inverse[...], (pending[...] - received[...].astype(F32)).astype(BF16)).astype(BF16)


def solve_last_body(pending, received, inverse, answered):
    solved = dot(inverse[...], (pending[...] - received[...].astype(F32)).astype(BF16)).astype(BF16)
    answered[...] = lax.dot_general(
        solved, inverse[...], (((0,), (0,)), ((), ())), preferred_element_type=F32
    ).astype(BF16)


def solve(body, pending, received, inverse):
    shape = jax.ShapeDtypeStruct(pending.shape, BF16)
    return call(body, shape, [VMEM] * 3, VMEM, limit=8, flops=1 << 25, moved=1 << 20)(
        pending, received, inverse
    )


def back_product(places, slot, x_rows, pair):
    total = dot(x_rows[places[slot]], pair[0])
    return (total + dot(x_rows[places[slot + 1]], pair[1])).astype(BF16)


def far_back_body(level, zero, places, own, other, tiles, *refs):
    x_rows, outs = refs[-4], refs[-3:]
    if zero:
        x_rows[x_rows.shape[0] - 1] = jnp.zeros_like(own)
    x_rows[2 * level] = own[...]
    x_rows[2 * level + 1] = other[...]
    for i in range(12):
        outs[i // 4][i % 4] = back_product(places, 64 * level + 40 + 2 * i, x_rows, tiles[i])


def far_back(level, levels, places, own, other, tiles, x_rows):
    cases, size = own.shape
    zero = x_rows is None
    part = jax.ShapeDtypeStruct((4, cases, size), BF16)
    args = [places, own, other, tiles] + ([] if zero else [x_rows])
    return call(
        partial(far_back_body, level, zero),
        [jax.ShapeDtypeStruct((2 * levels - 1, cases, size), BF16), part, part, part],
        [SMEM] + [VMEM] * (len(args) - 1),
        [VMEM] * 4,
        aliases={} if zero else {4: 0},
        limit=16,
        flops=48 * size * size * cases,
        moved=1 << 20,
    )(*args)


def near_back_body(level, order, places, x_rows, solved, tiles, inverses, out, turned, inverse, *refs):
    buf, sems = refs[-2:]
    copies = fetch(tiles, level, order, 16, 4, buf, sems)
    later = [bring(inverses, level, inverse, sems.at[16])]
    if level:
        later += fetch(tiles, level - 1, order, 20, 12, refs[0], sems, 4)
    turned[...] = solved[...].T
    for copy in copies:
        copy.wait()
    for i in range(4):
        out[i] = back_product(places, 64 * level + 32 + 2 * i, x_rows, buf[i])
    for copy in later:
        copy.wait()


def near_back(level, order, places, x_rows, solved, tiles, inverses):
    cases, size = x_rows.shape[1:]
    out = [
        jax.ShapeDtypeStruct((4, cases, size), BF16),
        jax.ShapeDtypeStruct((cases, size), BF16),
        jax.ShapeDtypeStruct((size, size), BF16),
    ]
    if level:
        out.append(jax.ShapeDtypeStruct((12, 2, size, size), BF16))
    return call(
        partial(near_back_body, level),
        out,
        [SMEM, SMEM, VMEM, VMEM, HBM, HBM],
        [VMEM] * len(out),
        [pltpu.VMEM((4, 2, size, size), BF16), pltpu.SemaphoreType.DMA((17,))],
        flops=16 * size * size * cases,
        moved=64 * size * size,
    )(order, places, x_rows, solved, tiles, inverses)


def add_body(a, b, c, d, *outs):
    for i in range(4):
        total = a[i].astype(F32) + b[i].astype(F32) + c[i].astype(F32) + d[i].astype(F32)
        outs[i][...] = total.astype(BF16)


def add_four(parts):
    shape = jax.ShapeDtypeStruct(parts[0].shape[1:], BF16)
    return call(add_body, [shape] * 4, [VMEM] * 4, [VMEM] * 4, limit=8, flops=1 << 20, moved=1 << 21)(*parts)


def answer_body(solved, own, a, b, c, inverse, out):
    term = own[...].astype(F32) + a[...].astype(F32) + b[...].astype(F32) + c[...].astype(F32)
    out[...] = dot((solved[...].astype(F32) - term).astype(BF16), inverse[...]).astype(BF16)


def answer(solved, own, received, inverse):
    shape = jax.ShapeDtypeStruct(solved.shape, BF16)
    return call(answer_body, shape, [VMEM] * 6, VMEM, limit=8, flops=1 << 25, moved=1 << 20)(
        solved, own, *received, inverse
    )


def shards(load_cases, diag_inverse, factor_tiles, targets, tile_live):
    levels = load_cases.shape[0]
    size, cases = load_cases.shape[3:]
    y, x, c = (lax.axis_index(name) for name in AXES)

    def order_of(sign, groups, blocks):
        far, near = jnp.array(groups, jnp.int32)[:, None], jnp.array(blocks, jnp.int32)[None, :]
        ys = jnp.where(c == 0, y + sign * far + 0 * near, y + sign * near + 0 * far) % 4
        xs = jnp.where(c == 0, x + sign * near + 0 * far, x + sign * far + 0 * near) % 4
        return (ys * 4 + xs).reshape(-1)

    level_ids = jnp.arange(levels - 1, dtype=jnp.int32)[:, None, None]
    owner = targets[:, 0]
    places = 2 * (level_ids + owner // 2) + ((owner % 2) ^ c)
    places = jnp.where(tile_live[:, 0] > 0, places, 2 * (levels - 1))
    order = jnp.concatenate([order_of(-1, FAR, NEAR), order_of(1, OUT, OUT)])
    places = places[:, order].reshape(-1)

    solved = [solve_first(load_cases, diag_inverse)]
    acc = None
    for height in range(levels - 1):
        mine = solved[height]
        group = jnp.stack([mine] + [send(mine, True, s) for s in NEAR[1:]])
        far_groups = [send(group, False, s) for s in FAR[1:]]
        last = height == levels - 2
        acc, ahead, load, inverse, *rest = near_fold(
            height, order, places, group, factor_tiles, load_cases, diag_inverse, acc, last
        )
        acc = mid_fold(height, places, far_groups[2], ahead, acc)
        acc, pending, outgoing = far_fold(height, places, far_groups[:2], ahead, load, acc)
        body = solve_last_body if last else solve_body
        solved.append(solve(body, pending, swap_cores(outgoing), inverse))

    latest = solved[-1]
    results = [latest]
    x_rows = None
    for height in reversed(range(levels - 1)):
        x_rows, *parts = far_back(
            height, levels, places, latest, swap_cores(latest), rest[0], x_rows
        )
        moved = [send(part, False, s) for part, s in zip(parts, OUT[1:])]
        kept, turned, inverse, *rest = near_back(
            height, order, places, x_rows, solved[height], factor_tiles, diag_inverse
        )
        own, *others = add_four([kept] + moved)
        received = [send(other, True, s) for other, s in zip(others, OUT[1:])]
        latest = answer(turned, own, received, inverse)
        results.append(latest)
    results = lax.optimization_barrier(tuple(reversed(results)))
    return jnp.stack([result.T for result in results])[:, None, None]


def solution(mesh):
    devices = mesh.devices
    split = Mesh(devices.reshape((4, 4) + devices.shape[1:]), ("y", "x", "col", "rhs"))
    row = ("y", "x")
    return jax.shard_map(
        shards,
        mesh=split,
        in_specs=(
            P(None, "col", row, None, "rhs"),
            P(None, "col", row, None, None),
            P(None, "col", None, row, None, None),
            P(None, "col", None, row),
            P(None, "col", None, row),
        ),
        out_specs=P(None, "col", row, None, "rhs"),
        check_vma=False,
    )
```

```python
from functools import partial

import jax
import jax.numpy as jnp
import numpy as np
from jax import lax
from jax.experimental import pallas as pl
from jax.experimental.pallas import tpu as pltpu
from jax.sharding import Mesh, PartitionSpec as P

F32, BF16 = jnp.float32, jnp.bfloat16
AXES = ("y", "x", "col")
NEAR = (0, 2, 1, 3)
FAR = (0, 1, 3, 2)
OUT = (0, 2, 1, 3)
VMEM = pl.BlockSpec(memory_space=pltpu.VMEM)
SMEM = pl.BlockSpec(memory_space=pltpu.SMEM)
HBM = pl.BlockSpec(memory_space=pltpu.HBM)


def pairs(near, shift):
    out = []
    for y in range(4):
        for x in range(4):
            for c in range(2):
                on_x = (c == 0) == near
                ty, tx = (y, (x + shift) % 4) if on_x else ((y + shift) % 4, x)
                out.append(((y * 4 + x) * 2 + c, (ty * 4 + tx) * 2 + c))
    return out


def send(value, near, shift):
    return lax.ppermute(value, AXES, pairs(near, shift))


def swap_cores(value):
    return lax.ppermute(value, "col", [(0, 1), (1, 0)])


def call(body, out, in_specs, out_specs, scratch=(), aliases={}, flops=0, moved=0, limit=40):
    return pl.pallas_call(
        body,
        out_shape=out,
        in_specs=in_specs,
        out_specs=out_specs,
        scratch_shapes=list(scratch),
        input_output_aliases=aliases,
        compiler_params=pltpu.CompilerParams(vmem_limit_bytes=limit << 20),
        cost_estimate=pl.CostEstimate(flops=flops, bytes_accessed=moved, transcendentals=0),
    )


def dot(a, b):
    return jnp.dot(a, b, preferred_element_type=F32)


def fetch(tiles, level, order, first, count, buf, sems, base=0):
    copies = [
        pltpu.make_async_copy(tiles.at[level, 0, order[first + i]], buf.at[i], sems.at[base + i])
        for i in range(count)
    ]
    for copy in copies:
        copy.start()
    return copies


def bring(source, level, target, sem):
    copy = pltpu.make_async_copy(source.at[level, 0, 0], target, sem)
    copy.start()
    return copy


def first_body(loads, inverses, solved, load, inverse, sems):
    copies = [bring(loads, 0, load, sems.at[0]), bring(inverses, 0, inverse, sems.at[1])]
    for copy in copies:
        copy.wait()
    solved[...] = dot(inverse[...], load[...]).astype(BF16)


def solve_first(loads, inverses):
    shape = loads.shape[3:]
    return call(
        first_body,
        jax.ShapeDtypeStruct(shape, BF16),
        [HBM] * 2,
        VMEM,
        [pltpu.VMEM(shape, BF16), pltpu.VMEM(inverses.shape[3:], BF16), pltpu.SemaphoreType.DMA((2,))],
        flops=1 << 25,
        moved=1 << 19,
    )(loads, inverses)


def add_products(places, base, blocks, buf, acc):
    size = acc.shape[1]
    for i in range(4 * len(blocks)):
        product = dot(buf[i].reshape(2 * size, size), blocks[i // 4][i % 4])
        for k in range(2):
            acc[places[base + 2 * i + k]] += product[k * size : (k + 1) * size]


def near_fold_body(level, zero, after, *refs):
    refs = list(refs)
    order, places, block, tiles, loads, inverses = refs[:6]
    refs = refs[6:]
    if not zero:
        refs.pop(0)
    acc, ahead, load, inverse = refs[:4]
    buf, sems = refs[-2:]
    copies = fetch(tiles, level, order, 0, 4, buf, sems)
    later = fetch(tiles, level, order, 4, 12, ahead, sems, 4)
    later.append(bring(loads, level + 1, load, sems.at[28]))
    later.append(bring(inverses, level + 1, inverse, sems.at[29]))
    if after:
        later += fetch(tiles, level, order, 20, 12, refs[4], sems, 16)
    if zero:
        acc[...] = jnp.zeros_like(acc)
    for copy in copies:
        copy.wait()
    add_products(places, 64 * level, [block], buf, acc)
    for copy in later:
        copy.wait()


def near_fold(level, order, places, block, tiles, loads, inverses, acc, after):
    size, cases = block.shape[1:]
    levels = tiles.shape[0]
    zero = acc is None
    out = [
        jax.ShapeDtypeStruct((2 * levels + 1, size, cases), F32),
        jax.ShapeDtypeStruct((12, 2, size, size), BF16),
        jax.ShapeDtypeStruct((size, cases), BF16),
        jax.ShapeDtypeStruct((size, size), BF16),
    ]
    if after:
        out.append(out[1])
    args = [order, places, block, tiles, loads, inverses]
    specs = [SMEM, SMEM, VMEM, HBM, HBM, HBM]
    if not zero:
        args.append(acc)
        specs.append(VMEM)
    return call(
        partial(near_fold_body, level, zero, after),
        out,
        specs,
        [VMEM] * len(out),
        [pltpu.VMEM((4, 2, size, size), BF16), pltpu.SemaphoreType.DMA((30,))],
        {} if zero else {6: 0},
        flops=16 * size * size * cases,
        moved=64 * size * size,
    )(*args)


def mid_fold_body(level, places, block, tiles, _, acc):
    add_products(places, 64 * level + 24, [block], tiles.at[8:12], acc)


def mid_fold(level, places, block, tiles, acc):
    size = block.shape[1]
    return call(
        partial(mid_fold_body, level),
        jax.ShapeDtypeStruct(acc.shape, F32),
        [SMEM] + [VMEM] * 3,
        VMEM,
        aliases={3: 0},
        limit=16,
        flops=16 * size * size * size,
        moved=1 << 20,
    )(places, block, tiles, acc)


def far_fold_body(level, places, a, b, tiles, load, _, acc, pending, outgoing):
    add_products(places, 64 * level + 8, [a, b], tiles, acc)
    pending[...] = load[...].astype(F32) - acc[2 * level]
    outgoing[...] = acc[2 * level + 1].astype(BF16)


def far_fold(level, places, blocks, tiles, load, acc):
    size, cases = load.shape
    half = jax.ShapeDtypeStruct((size, cases), F32)
    return call(
        partial(far_fold_body, level),
        [jax.ShapeDtypeStruct(acc.shape, F32), half, jax.ShapeDtypeStruct((size, cases), BF16)],
        [SMEM] + [VMEM] * 5,
        [VMEM] * 3,
        aliases={5: 0},
        limit=16,
        flops=48 * size * size * cases,
        moved=1 << 20,
    )(places, *blocks, tiles, load, acc)


def solve_body(pending, received, inverse, solved):
    solved[...] = dot(inverse[...], (pending[...] - received[...].astype(F32)).astype(BF16)).astype(BF16)


def solve_last_body(pending, received, inverse, answered):
    solved = dot(inverse[...], (pending[...] - received[...].astype(F32)).astype(BF16)).astype(BF16)
    answered[...] = lax.dot_general(
        solved, inverse[...], (((0,), (0,)), ((), ())), preferred_element_type=F32
    ).astype(BF16)


def solve(body, pending, received, inverse):
    shape = jax.ShapeDtypeStruct(pending.shape, BF16)
    return call(body, shape, [VMEM] * 3, VMEM, limit=8, flops=1 << 25, moved=1 << 20)(
        pending, received, inverse
    )


def back_product(places, slot, x_rows, pair):
    total = dot(x_rows[places[slot]], pair[0])
    return (total + dot(x_rows[places[slot + 1]], pair[1])).astype(BF16)


def far_back_body(level, zero, places, own, other, tiles, *refs):
    x_rows, outs = refs[-4], refs[-3:]
    if zero:
        x_rows[x_rows.shape[0] - 1] = jnp.zeros_like(own)
    x_rows[2 * level] = own[...]
    x_rows[2 * level + 1] = other[...]
    for i in range(12):
        outs[i // 4][i % 4] = back_product(places, 64 * level + 40 + 2 * i, x_rows, tiles[i])


def far_back(level, levels, places, own, other, tiles, x_rows):
    cases, size = own.shape
    zero = x_rows is None
    part = jax.ShapeDtypeStruct((4, cases, size), BF16)
    args = [places, own, other, tiles] + ([] if zero else [x_rows])
    return call(
        partial(far_back_body, level, zero),
        [jax.ShapeDtypeStruct((2 * levels - 1, cases, size), BF16), part, part, part],
        [SMEM] + [VMEM] * (len(args) - 1),
        [VMEM] * 4,
        aliases={} if zero else {4: 0},
        limit=16,
        flops=48 * size * size * cases,
        moved=1 << 20,
    )(*args)


def near_back_body(
    level, order, places, x_rows, solved, tiles, inverses, out, turned, inverse, upright, *refs
):
    buf, sems = refs[-2:]
    copies = fetch(tiles, level, order, 16, 4, buf, sems)
    later = [bring(inverses, level, inverse, sems.at[16])]
    if level:
        later += fetch(tiles, level - 1, order, 20, 12, refs[0], sems, 4)
    turned[...] = solved[...].T
    upright[...] = x_rows[2 * level].T
    for copy in copies:
        copy.wait()
    for i in range(4):
        out[i] = back_product(places, 64 * level + 32 + 2 * i, x_rows, buf[i])
    for copy in later:
        copy.wait()


def near_back(level, order, places, x_rows, solved, tiles, inverses):
    cases, size = x_rows.shape[1:]
    out = [
        jax.ShapeDtypeStruct((4, cases, size), BF16),
        jax.ShapeDtypeStruct((cases, size), BF16),
        jax.ShapeDtypeStruct((size, size), BF16),
        jax.ShapeDtypeStruct((size, cases), BF16),
    ]
    if level:
        out.append(jax.ShapeDtypeStruct((12, 2, size, size), BF16))
    return call(
        partial(near_back_body, level),
        out,
        [SMEM, SMEM, VMEM, VMEM, HBM, HBM],
        [VMEM] * len(out),
        [pltpu.VMEM((4, 2, size, size), BF16), pltpu.SemaphoreType.DMA((17,))],
        flops=16 * size * size * cases,
        moved=64 * size * size,
    )(order, places, x_rows, solved, tiles, inverses)


def add_body(a, b, c, d, *outs):
    for i in range(4):
        total = a[i].astype(F32) + b[i].astype(F32) + c[i].astype(F32) + d[i].astype(F32)
        outs[i][...] = total.astype(BF16)


def add_four(parts):
    shape = jax.ShapeDtypeStruct(parts[0].shape[1:], BF16)
    return call(add_body, [shape] * 4, [VMEM] * 4, [VMEM] * 4, limit=8, flops=1 << 20, moved=1 << 21)(*parts)


def answer_body(upright, solved, own, a, b, c, inverse, out):
    term = own[...].astype(F32) + a[...].astype(F32) + b[...].astype(F32) + c[...].astype(F32)
    answered = dot((solved[...].astype(F32) - term).astype(BF16), inverse[...]).astype(BF16)
    out[...] = answered.T if upright else answered


def answer(solved, own, received, inverse, upright):
    shape = jax.ShapeDtypeStruct(solved.shape[::-1] if upright else solved.shape, BF16)
    return call(partial(answer_body, upright), shape, [VMEM] * 6, VMEM, limit=8, flops=1 << 25, moved=1 << 20)(
        solved, own, *received, inverse
    )


def shards(load_cases, diag_inverse, factor_tiles, targets, tile_live):
    levels = load_cases.shape[0]
    size, cases = load_cases.shape[3:]
    y, x, c = (lax.axis_index(name) for name in AXES)

    def order_of(sign, groups, blocks):
        far, near = jnp.array(groups, jnp.int32)[:, None], jnp.array(blocks, jnp.int32)[None, :]
        ys = jnp.where(c == 0, y + sign * far + 0 * near, y + sign * near + 0 * far) % 4
        xs = jnp.where(c == 0, x + sign * near + 0 * far, x + sign * far + 0 * near) % 4
        return (ys * 4 + xs).reshape(-1)

    level_ids = jnp.arange(levels - 1, dtype=jnp.int32)[:, None, None]
    owner = targets[:, 0]
    places = 2 * (level_ids + owner // 2) + ((owner % 2) ^ c)
    places = jnp.where(tile_live[:, 0] > 0, places, 2 * (levels - 1))
    order = jnp.concatenate([order_of(-1, FAR, NEAR), order_of(1, OUT, OUT)])
    places = places[:, order].reshape(-1)

    solved = [solve_first(load_cases, diag_inverse)]
    acc = None
    for height in range(levels - 1):
        mine = solved[height]
        group = jnp.stack([mine] + [send(mine, True, s) for s in NEAR[1:]])
        far_groups = [send(group, False, s) for s in FAR[1:]]
        last = height == levels - 2
        acc, ahead, load, inverse, *rest = near_fold(
            height, order, places, group, factor_tiles, load_cases, diag_inverse, acc, last
        )
        acc = mid_fold(height, places, far_groups[2], ahead, acc)
        acc, pending, outgoing = far_fold(height, places, far_groups[:2], ahead, load, acc)
        body = solve_last_body if last else solve_body
        solved.append(solve(body, pending, swap_cores(outgoing), inverse))

    latest = solved[-1]
    results = []
    x_rows = None
    for height in reversed(range(levels - 1)):
        x_rows, *parts = far_back(
            height, levels, places, latest, swap_cores(latest), rest[0], x_rows
        )
        moved = [send(part, False, s) for part, s in zip(parts, OUT[1:])]
        kept, turned, inverse, upright, *rest = near_back(
            height, order, places, x_rows, solved[height], factor_tiles, diag_inverse
        )
        own, *others = add_four([kept] + moved)
        received = [send(other, True, s) for other, s in zip(others, OUT[1:])]
        latest = answer(turned, own, received, inverse, height == 0)
        results.append(upright)
    results = lax.optimization_barrier((latest, *reversed(results)))
    return jnp.stack(results)[:, None, None]


def solution(mesh):
    devices = mesh.devices
    split = Mesh(devices.reshape((4, 4) + devices.shape[1:]), ("y", "x", "col", "rhs"))
    row = ("y", "x")
    return jax.shard_map(
        shards,
        mesh=split,
        in_specs=(
            P(None, "col", row, None, "rhs"),
            P(None, "col", row, None, None),
            P(None, "col", None, row, None, None),
            P(None, "col", None, row),
            P(None, "col", None, row),
        ),
        out_specs=P(None, "col", row, None, "rhs"),
        check_vma=False,
    )
```
